256 devices in a mesh: occ: 16 (over x, z_hi, core), vir: 16 (over y, z_lo).
Axes of the slice: x: 4, y: 4, z: 8 (z_hi: 2, z_lo: 4; z = z_hi * 4 + z_lo), core: 2. Of those that a mesh axis runs over, the one named last changes fastest.
Arguments:
- amplitudes: bfloat16 [16384, 2048], P('occ', 'vir'), may hold values from -6 to 6
- integrals: bfloat16 [2048, 32768], P('occ', 'vir'), may hold values from -0.25 to 0.25
- contract_class: int32 [16], replicated, may hold values from 0 to 7, as said below
- column_class: int32 [256], P('vir'), may hold values from 0 to 7, as said below
Outputs:
- residual: float32 [16384, 32768], P('occ', 'vir')
The draws below stay inside these ranges and needn't reach their ends.
Inputs may be any that keep to these rules, and one draw needn't show every extreme that they name: `contract_class`: each class 0 to 7 labels exactly 2 of the contracted pair tiles. `column_class`: every class 0 to 7 occurs among the tiles; the 16 tiles of one index of vir may all share one class.
All inputs are finite; a program needn't handle non-finite values.
Results may differ from the reference program's by a relative error of at most 0.0003.
Values may be sent and summed in bfloat16 or wider, within the bound.
No kernel may reach another device: no remote copies, remote signals or barrier semaphores. Data moves between devices by JAX's collectives and lax.ppermute only.
A program may use at most 128 MiB of HBM per device.

```python
import jax
import jax.numpy as jnp

P_SIZE = 128
SYMS = 8
NK = 16
LT_DEV = 16
NL = 256
ROWS = 16384


def draw_contract_class(key, part):
    key = jax.random.fold_in(key, 11)
    labels = jnp.tile(jnp.arange(SYMS, dtype=jnp.int32), NK // SYMS)
    shuffle = jax.random.permutation(key, NK)
    return labels[shuffle].astype(jnp.int32)


def draw_column_class(key, part):
    key = jax.random.fold_in(key, 23)
    first_key, second_key, place_key, block_key, class_key = jax.random.split(key, 5)
    lower_draw = jax.random.randint(first_key, (NL,), 0, SYMS, dtype=jnp.int32)
    upper_draw = jax.random.randint(second_key, (NL,), 0, SYMS, dtype=jnp.int32)
    labels = jnp.minimum(lower_draw, upper_draw)
    groups = NL // LT_DEV
    chosen = jax.random.randint(block_key, (), 0, groups, dtype=jnp.int32)
    single = jax.random.randint(class_key, (), 0, SYMS, dtype=jnp.int32)
    others = jnp.arange(NL - LT_DEV, dtype=jnp.int32)
    others = jnp.where(others < chosen * LT_DEV, others, others + LT_DEV)
    picked = jax.random.permutation(place_key, others)[:SYMS]
    labels = labels.at[picked].set(jnp.arange(SYMS, dtype=jnp.int32))
    position = jnp.arange(NL, dtype=jnp.int32)
    labels = jnp.where(position // LT_DEV == chosen, single, labels)
    return labels.astype(jnp.int32)


def block_levels(stream_key, extent, cuts, low, top_value):
    level, own = 1.0, jax.random.fold_in(stream_key, 6)
    for dim, blocks in cuts:
        heights = jnp.exp(jax.random.uniform(jax.random.fold_in(own, dim), (blocks,), jnp.float32, low / len(cuts), top_value / len(cuts)))
        level = level * jnp.repeat(heights, extent[dim] // blocks).reshape([-1 if axis == dim else 1 for axis in range(len(extent))])
    return level


def gaussian(own_key, extent, scale, bound, cuts=(), held_as=jnp.bfloat16):
    gain = block_levels(own_key, extent, cuts, -0.22, 0.18) if cuts else 1.0
    entries = jax.random.normal(own_key, extent, jnp.float32) * scale * gain
    return jnp.minimum(jnp.maximum(entries, -bound), bound).astype(held_as)


def setup_inputs(seed: int = 0) -> dict:
    arg_keys = jax.random.split(jax.random.key(seed), 5)
    amplitudes = gaussian(arg_keys[0], (ROWS, NK * P_SIZE), 1.0, 6.0, ((0, 16), (1, 16)))
    integrals = gaussian(arg_keys[1], (NK * P_SIZE, NL * P_SIZE), (NK * P_SIZE // 4) ** -0.5, 0.25, ((0, 16), (1, 16)))
    contract_class = draw_contract_class(jax.random.fold_in(arg_keys[4], 71), 0)
    column_class = draw_column_class(jax.random.fold_in(arg_keys[4], 71), 0)
    return {"amplitudes": amplitudes, "integrals": integrals, "contract_class": contract_class, "column_class": column_class}


def reference(amplitudes, integrals, contract_class, column_class):
    match = contract_class[:, None] == column_class[None, :]
    shaped = integrals.reshape(NK, P_SIZE, NL, P_SIZE)
    kept = jnp.where(match[:, None, :, None], shaped, jnp.zeros_like(shaped)).reshape(NK * P_SIZE, NL * P_SIZE)
    return jnp.dot(amplitudes, kept, preferred_element_type=jnp.float32)
```

```python
import functools

import jax
import jax.numpy as jnp
from jax import lax
from jax.experimental import pallas as pl
from jax.experimental.pallas import tpu as pltpu
from jax.sharding import Mesh, PartitionSpec as P

P_SIZE = 128
OCC = ("x", "zh", "core")
VIR = ("y", "zl")
NY = 4
NZ = 4


def multiply_kernel(spots, slots, *refs):
    pieces, slab_ref = refs[: len(spots)], refs[len(spots)]
    out_ref, amps, sems = refs[len(spots) + 1 :]

    @pl.when(pl.program_id(0) == 0)
    def _():
        copies = [
            pltpu.make_async_copy(
                piece, amps.at[slot, pl.ds(start, piece.shape[0])], sems.at[i]
            )
            for i, (piece, (slot, start)) in enumerate(zip(pieces, spots))
        ]
        for copy in copies:
            copy.start()
        for copy in copies:
            copy.wait()

    l = pl.program_id(0)
    pair = jnp.concatenate([amps[slots[0, l]], amps[slots[1, l]]], axis=1)
    out_ref[...] = jnp.dot(pair, slab_ref[...], preferred_element_type=jnp.float32)


def multiply(slots, spots, pieces, slab):
    rows = pieces[0].shape[0]
    depth, width = slab.shape
    tiles = width // P_SIZE
    return pl.pallas_call(
        functools.partial(multiply_kernel, spots),
        out_shape=jax.ShapeDtypeStruct((rows, width), jnp.float32),
        grid_spec=pltpu.PrefetchScalarGridSpec(
            num_scalar_prefetch=1,
            grid=(tiles,),
            in_specs=[pl.BlockSpec(memory_space=pl.ANY)] * len(pieces)
            + [pl.BlockSpec((depth, P_SIZE), lambda l, slots: (0, l))],
            out_specs=pl.BlockSpec((rows, P_SIZE), lambda l, slots: (0, l)),
            scratch_shapes=[
                pltpu.VMEM((NY * NZ, rows, P_SIZE), jnp.bfloat16),
                pltpu.SemaphoreType.DMA((len(pieces),)),
            ],
        ),
        compiler_params=pltpu.CompilerParams(vmem_limit_bytes=32 * 1024 * 1024),
        cost_estimate=pl.CostEstimate(
            flops=2 * rows * depth * width,
            bytes_accessed=4 * rows * width + 2 * rows * P_SIZE * NY * NZ,
            transcendentals=0,
        ),
    )(slots, *pieces, slab)


def shift(value, axis, step, size):
    return lax.ppermute(value, axis, [(i, (i - step) % size) for i in range(size)])


def swap(value, axis, bit, size):
    return lax.ppermute(value, axis, [(i, i ^ bit) for i in range(size)])


def gather_pieces(own):
    half = own.shape[0] // 2
    line = [own] + [swap(own, "zl", bit, NZ) for bit in range(1, NZ)]
    spots, pieces = [], []
    for dz, block in enumerate(line):
        up = shift(block, "y", 1, NY)
        down = shift(block, "y", -1, NY)
        far_top = shift(up[:half], "y", 1, NY)
        far_bottom = shift(down[half:], "y", -1, NY)
        spots += [(dz, 0), (NZ + dz, 0), (3 * NZ + dz, 0)]
        spots += [(2 * NZ + dz, 0), (2 * NZ + dz, half)]
        pieces += [block, up, down, far_top, far_bottom]
    return tuple(spots), pieces


def body(amplitudes, integrals, contract_class, column_class):
    nk = contract_class.shape[0]
    me = lax.axis_index(OCC)
    y, z = lax.axis_index("y"), lax.axis_index("zl")

    same = contract_class[:, None] == contract_class[None, :]
    order = jnp.arange(nk, dtype=jnp.int32)
    rank = jnp.sum(same & (order[None, :] < order[:, None]), axis=1)
    mine, my_rank = contract_class[me], rank[me]
    hit = jnp.repeat(column_class == mine, P_SIZE)[None, None, :]
    place = (jnp.arange(2) == my_rank)[:, None, None]
    slab = jnp.where(hit & place, integrals[None], jnp.zeros_like(integrals)[None])
    slab = lax.psum(slab.reshape(2 * P_SIZE, -1), OCC)

    match = contract_class[None, :, None] == column_class[None, None, :]
    match = match & (rank[None, :, None] == jnp.arange(2)[:, None, None])
    slot = ((order // NZ - y) % NY) * NZ + ((order % NZ) ^ z)
    slots = jnp.sum(jnp.where(match, slot[None, :, None], 0), axis=1).astype(jnp.int32)

    spots, pieces = gather_pieces(amplitudes)
    return multiply(slots, spots, pieces, slab)


def solution(mesh):
    fine = Mesh(mesh.devices.reshape(4, 2, 2, NY, NZ), OCC + VIR)
    placed = (P(OCC, VIR), P(OCC, VIR), P(), P(VIR))
    return jax.shard_map(
        body, mesh=fine, in_specs=placed, out_specs=P(OCC, VIR), check_vma=False
    )
```

```python
import functools

import jax
import jax.numpy as jnp
from jax import lax
from jax.experimental import pallas as pl
from jax.experimental.pallas import tpu as pltpu
from jax.sharding import Mesh, PartitionSpec as P

P_SIZE = 128
SYMS = 8
OCC = ("x", "zh", "core")
VIR = ("y", "zl")
NX = NY = NZ = 4
NK = 16
QUARTER = 4
STEP = 256

SLOTS = 0
MERGE = 2 * NK
HALVES = MERGE + 2 * QUARTER
TABLE = HALVES + 2 * QUARTER

VMEM = pl.BlockSpec(memory_space=pltpu.VMEM)
SMEM = pl.BlockSpec(memory_space=pltpu.SMEM)
ANY = pl.BlockSpec(memory_space=pl.ANY)


def swap_cores(value):
    return lax.ppermute(value, "core", [(0, 1), (1, 0)])


def ring(value):
    pairs = []
    for y in range(NY):
        pairs += [(y, (y + 1) % NY), (NY + y, NY + (y - 1) % NY)]
    return lax.ppermute(value, ("core", "y"), pairs)


def cross_x(value, bits):
    pairs = [(2 * x + c, 2 * (x ^ bits[c]) + c) for x in range(NX) for c in range(2)]
    return lax.ppermute(value, ("x", "core"), pairs)


def cross_z(value, bits):
    pairs = [(NZ * c + z, NZ * c + (z ^ bits[c])) for z in range(NZ) for c in range(2)]
    return lax.ppermute(value, ("core", "zl"), pairs)


def table_kernel(contract, column, out, inverse, rank, chosen):
    x, zh, c = (lax.axis_index(axis) for axis in OCC)
    y, z = (lax.axis_index(axis) for axis in VIR)
    one, two = (y + 3 + 2 * c) % NY, (y + 1 + 2 * c) % NY
    far = (y + 2) % NY
    near, other = z ^ (1 + c), z ^ (2 - c)
    sources = [
        (y, z), (y, near), (y, other), (y, z ^ 3),
        (one, z), (two, z), (far, z),
        (one, near), (two, other), (one, other), (two, near),
        (one, z ^ 3), (two, z ^ 3),
        (far, z ^ 1), (far, z ^ 2), (far, z ^ 3),
    ]
    for i, (row, col) in enumerate(sources):
        inverse[row * NZ + col] = i
    for s in range(SYMS):
        chosen[2 * SYMS + s] = 0
    for k in range(NK):
        label = contract[k]
        place = chosen[2 * SYMS + label]
        rank[k] = place
        chosen[2 * label + place] = inverse[k]
        chosen[2 * SYMS + label] = place + 1
    for l in range(NK):
        for r in range(2):
            out[SLOTS + r * NK + l] = chosen[2 * column[l] + r]

    near_x = x ^ (1 + 2 * c)
    tiles = [
        x * 4 + zh * 2 + c,
        near_x * 4 + zh * 2 + c,
        near_x * 4 + zh * 2 + 1 - c,
        (x ^ 2) * 4 + zh * 2 + c,
    ]
    for j in range(QUARTER):
        half = c if j < 2 else 1 - c
        label = column[QUARTER * x + 2 * half + j % 2]
        for r in range(2):
            found = jnp.int32(len(tiles))
            for s, tile in enumerate(tiles):
                hit = (contract[tile] == label) & (rank[tile] == r)
                found = jnp.where(hit, s, found)
            out[MERGE + r * QUARTER + j] = found

    far_x = x ^ (3 - 2 * c)
    halves = [
        (x, c), (x, 1 - c),
        (near_x, c), (near_x, 1 - c),
        (far_x, 1 - c), (far_x, c),
        (x ^ 2, c), (x ^ 2, 1 - c),
    ]
    for i, (quarter, half) in enumerate(halves):
        out[HALVES + 2 * quarter + half] = i


def make_table(contract_class, column_class):
    return pl.pallas_call(
        table_kernel,
        out_shape=jax.ShapeDtypeStruct((TABLE,), jnp.int32),
        in_specs=[SMEM, SMEM],
        out_specs=SMEM,
        scratch_shapes=[
            pltpu.SMEM((NK,), jnp.int32),
            pltpu.SMEM((NK,), jnp.int32),
            pltpu.SMEM((3 * SYMS,), jnp.int32),
        ],
    )(contract_class, column_class)


def cut_kernel(integrals, own, near, far, across, sems):
    x, c = lax.axis_index("x"), lax.axis_index("core")
    width = own.shape[1]
    quarters = [x, x ^ (1 + 2 * c), x ^ (3 - 2 * c), x ^ 2]
    copies = []
    for i, (quarter, out) in enumerate(zip(quarters, (own, near, far, across))):
        columns = pl.ds(pl.multiple_of(quarter * width, width), width)
        copies.append(pltpu.make_async_copy(integrals.at[:, columns], out, sems.at[i]))
    for copy in copies:
        copy.start()
    for copy in copies:
        copy.wait()


def cut(integrals):
    depth, width = integrals.shape
    shape = jax.ShapeDtypeStruct((depth, width // NX), integrals.dtype)
    return pl.pallas_call(
        cut_kernel,
        out_shape=[shape] * 4,
        in_specs=[ANY],
        out_specs=[VMEM] * 4,
        scratch_shapes=[pltpu.SemaphoreType.DMA((4,))],
    )(integrals)


def merge_kernel(table, own, near, across, keep, send):
    tiles = [own, near.at[:P_SIZE], near.at[P_SIZE:], across]
    c = lax.axis_index("core")
    for j in range(QUARTER):
        half = c if j < 2 else 1 - c
        start = pl.multiple_of((2 * half + j % 2) * P_SIZE, P_SIZE)
        values = [tile[:, pl.ds(start, P_SIZE)] for tile in tiles]
        out = keep if j < 2 else send
        for r in range(2):
            found = table[MERGE + r * QUARTER + j]
            total = jnp.zeros_like(values[0])
            for s, value in enumerate(values):
                total = jnp.where(found == s, value, total)
            lane = (j % 2) * P_SIZE
            out[r * P_SIZE : (r + 1) * P_SIZE, lane : lane + P_SIZE] = total


def merge(table, own, near, across):
    shape = jax.ShapeDtypeStruct((2 * P_SIZE, 2 * P_SIZE), own.dtype)
    return pl.pallas_call(
        merge_kernel,
        out_shape=[shape] * 2,
        in_specs=[SMEM, VMEM, VMEM, VMEM],
        out_specs=[VMEM] * 2,
    )(table, own, near, across)


def make_slab(integrals, table):
    own, near, far, across = cut(integrals)
    near = jnp.concatenate([near, swap_cores(far)])
    near = cross_x(near, (1, 3))
    across = cross_x(across, (2, 2))
    keep, send = merge(table, own, near, across)
    part = keep + swap_cores(send)
    part = part + lax.ppermute(part, "zh", [(0, 1), (1, 0)])
    pair = jnp.concatenate([part, swap_cores(part)])
    near = cross_x(pair, (1, 3))
    across = cross_x(part, (2, 2))
    return [pair, near, swap_cores(near), across, swap_cores(across)]


def gather_amplitudes(own):
    rows = own.shape[0]
    pair = jnp.concatenate([own, swap_cores(own)])
    line = cross_z(pair, (1, 2))
    up0 = ring(pair)
    turned = swap_cores(line)
    up1 = ring(line)
    last = cross_z(line[:rows], (2, 1))
    far0 = ring(up0[:rows])
    up2 = ring(turned)
    up3 = ring(jnp.concatenate([last, swap_cores(last)]))
    far1 = cross_z(far0, (1, 1))
    far2 = cross_z(far0, (2, 2))
    far3 = ring(up3[:rows])
    down0 = swap_cores(up0[rows:])
    down1 = swap_cores(up1[rows:])
    down2 = swap_cores(up2[:rows])
    down3 = swap_cores(up3[rows:])
    return [
        (own, 0), (line, 0), (turned, rows), (last, 0),
        (up0, 0), (down0, 0), (far0, 0),
        (up1, 0), (down1, 0), (up2, rows), (down2, 0),
        (up3, 0), (down3, 0),
        (far1, 0), (far2, 0), (far3, 0),
    ]


def multiply_kernel(starts, table, *refs):
    pieces, refs = refs[:NK], refs[NK:]
    parts, (out, amps, slab, sems) = refs[:5], refs[5:]
    rows = amps.shape[1]

    @pl.when(pl.program_id(0) == 0)
    def _():
        copies = []
        for i, (piece, start) in enumerate(zip(pieces, starts)):
            source = piece.at[pl.ds(start, rows)]
            copies.append(pltpu.make_async_copy(source, amps.at[i], sems.at[i]))
        place = 0
        for i, part in enumerate(parts):
            size = part.shape[0]
            target = slab.at[pl.ds(place, size)]
            copies.append(pltpu.make_async_copy(part, target, sems.at[NK + i]))
            place += size
        for copy in copies:
            copy.start()
        for copy in copies:
            copy.wait()

    block = pl.ds(pl.multiple_of(pl.program_id(0) * STEP, STEP), STEP)
    depth = 2 * P_SIZE
    for l in range(NK):
        pair = jnp.concatenate(
            [amps[table[SLOTS + r * NK + l], block] for r in range(2)], axis=1
        )
        place = pl.multiple_of(table[HALVES + l // 2] * depth, depth)
        lane = (l % 2) * P_SIZE
        weights = slab[pl.ds(place, depth), lane : lane + P_SIZE]
        out[:, l * P_SIZE : (l + 1) * P_SIZE] = jnp.dot(
            pair, weights, preferred_element_type=jnp.float32
        )


def multiply(table, pieces, parts):
    rows = pieces[0][0].shape[0]
    width = NK * P_SIZE
    starts = tuple(start for _, start in pieces)
    return pl.pallas_call(
        functools.partial(multiply_kernel, starts),
        out_shape=jax.ShapeDtypeStruct((rows, width), jnp.float32),
        grid_spec=pltpu.PrefetchScalarGridSpec(
            num_scalar_prefetch=1,
            grid=(rows // STEP,),
            in_specs=[ANY] * (NK + len(parts)),
            out_specs=pl.BlockSpec((STEP, width), lambda i, table: (i, 0)),
            scratch_shapes=[
                pltpu.VMEM((NK, rows, P_SIZE), jnp.bfloat16),
                pltpu.VMEM((2 * NK * P_SIZE // 2, 2 * P_SIZE), jnp.bfloat16),
                pltpu.SemaphoreType.DMA((NK + len(parts),)),
            ],
        ),
        compiler_params=pltpu.CompilerParams(vmem_limit_bytes=24 * 1024 * 1024),
        cost_estimate=pl.CostEstimate(
            flops=4 * rows * P_SIZE * width,
            bytes_accessed=4 * rows * width,
            transcendentals=0,
        ),
    )(table, *[piece for piece, _ in pieces], *parts)


def body(amplitudes, integrals, contract_class, column_class):
    table = make_table(contract_class, column_class)
    pieces = gather_amplitudes(amplitudes)
    parts = make_slab(integrals, table)
    return multiply(table, pieces, parts)


def solution(mesh):
    fine = Mesh(mesh.devices.reshape(NX, 2, 2, NY, NZ), OCC + VIR)
    placed = (P(OCC, VIR), P(OCC, VIR), P(), P(VIR))
    return jax.shard_map(
        body, mesh=fine, in_specs=placed, out_specs=P(OCC, VIR), check_vma=False
    )
```

```python
import functools

import jax
import jax.numpy as jnp
from jax import lax
from jax.experimental import pallas as pl
from jax.experimental.pallas import tpu as pltpu
from jax.sharding import Mesh, PartitionSpec as P

P_SIZE = 128
SYMS = 8
OCC = ("x", "zh", "core")
VIR = ("y", "zl")
NX = NY = NZ = 4
NK = 16
QUARTER = 4
STEP = 256

SLOTS = 0
MERGE = 2 * NK
HALVES = MERGE + 2 * QUARTER
TABLE = HALVES + 2 * QUARTER

VMEM = pl.BlockSpec(memory_space=pltpu.VMEM)
SMEM = pl.BlockSpec(memory_space=pltpu.SMEM)
ANY = pl.BlockSpec(memory_space=pl.ANY)


def send(name, value, axes, pairs, *others):
    with jax.named_scope(name):
        if others:
            value = lax.optimization_barrier((value, *others))[0]
        return lax.ppermute(value, axes, pairs)


def swap(name, value, *others):
    return send(name, value, "core", [(0, 1), (1, 0)], *others)


def ring(name, value, *others):
    pairs = []
    for y in range(NY):
        pairs += [(y, (y + 1) % NY), (NY + y, NY + (y - 1) % NY)]
    return send(name, value, ("core", "y"), pairs, *others)


def cross_x(name, value, bits, *others):
    pairs = [(2 * x + c, 2 * (x ^ bits[c]) + c) for x in range(NX) for c in range(2)]
    return send(name, value, ("x", "core"), pairs, *others)


def after(value, *others):
    return lax.optimization_barrier((value, *others))[0]


def cross_z(name, value, bits, *others):
    pairs = [(NZ * c + z, NZ * c + (z ^ bits[c])) for z in range(NZ) for c in range(2)]
    return send(name, value, ("core", "zl"), pairs, *others)


def table_kernel(contract, column, out, inverse, rank, chosen):
    x, zh, c = (lax.axis_index(axis) for axis in OCC)
    y, z = (lax.axis_index(axis) for axis in VIR)
    one, two = (y + 3 + 2 * c) % NY, (y + 1 + 2 * c) % NY
    far = (y + 2) % NY
    sources = [(y, z), (y, z ^ 1), (y, z ^ 2), (y, z ^ 3)]
    for bit in range(NZ):
        sources += [(one, z ^ bit), (two, z ^ bit), (far, z ^ bit)]
    for i, (row, col) in enumerate(sources):
        inverse[row * NZ + col] = i
    for s in range(SYMS):
        chosen[2 * SYMS + s] = 0
    for k in range(NK):
        label = contract[k]
        place = chosen[2 * SYMS + label]
        rank[k] = place
        chosen[2 * label + place] = inverse[k]
        chosen[2 * SYMS + label] = place + 1
    for l in range(NK):
        for r in range(2):
            out[SLOTS + r * NK + l] = chosen[2 * column[l] + r]

    near_x, far_x = x ^ (1 + 2 * c), x ^ (3 - 2 * c)
    tiles = [
        x * 4 + zh * 2 + c,
        near_x * 4 + zh * 2 + c,
        near_x * 4 + zh * 2 + 1 - c,
        (x ^ 2) * 4 + zh * 2 + c,
    ]
    for j in range(QUARTER):
        half = c if j < 2 else 1 - c
        label = column[QUARTER * x + 2 * half + j % 2]
        for r in range(2):
            found = jnp.int32(len(tiles))
            for s, tile in enumerate(tiles):
                hit = (contract[tile] == label) & (rank[tile] == r)
                found = jnp.where(hit, s, found)
            out[MERGE + r * QUARTER + j] = found

    halves = [
        (x, c), (x, 1 - c),
        (near_x, c), (near_x, 1 - c),
        (x ^ 2, c),
        (far_x, 1 - c), (far_x, c),
        (x ^ 2, 1 - c),
    ]
    for i, (quarter, half) in enumerate(halves):
        out[HALVES + 2 * quarter + half] = i


def make_table(contract_class, column_class):
    return pl.pallas_call(
        table_kernel,
        out_shape=jax.ShapeDtypeStruct((TABLE,), jnp.int32),
        in_specs=[SMEM, SMEM],
        out_specs=SMEM,
        scratch_shapes=[
            pltpu.SMEM((NK,), jnp.int32),
            pltpu.SMEM((NK,), jnp.int32),
            pltpu.SMEM((3 * SYMS,), jnp.int32),
        ],
    )(contract_class, column_class)


def cut_kernel(integrals, *refs):
    outs, sems = refs[:NX], refs[NX]
    x, c = lax.axis_index("x"), lax.axis_index("core")
    half = outs[0].shape[1] // 2
    quarters = [(x, c), (x ^ (1 + 2 * c), c), (x ^ (3 - 2 * c), 1 - c), (x ^ 2, c)]
    copies = []
    for out, (quarter, first) in zip(outs, quarters):
        for i, side in enumerate((first, 1 - first)):
            start = pl.multiple_of((2 * quarter + side) * half, half)
            source = integrals.at[:, pl.ds(start, half)]
            target = out.at[:, pl.ds(i * half, half)]
            sem = sems.at[len(copies)]
            copies.append(pltpu.make_async_copy(source, target, sem))
    for copy in copies:
        copy.start()
    for copy in copies:
        copy.wait()


def cut(integrals):
    depth, width = integrals.shape
    shape = jax.ShapeDtypeStruct((depth, width // NX), integrals.dtype)
    return pl.pallas_call(
        cut_kernel,
        out_shape=[shape] * NX,
        in_specs=[ANY],
        out_specs=[VMEM] * NX,
        scratch_shapes=[pltpu.SemaphoreType.DMA((2 * NX,))],
    )(integrals)


def merge(table, tiles):
    found = table[MERGE : MERGE + 2 * QUARTER].reshape(2, 1, QUARTER)
    found = jnp.repeat(found, P_SIZE, axis=2)
    total = jnp.zeros_like(tiles[0])[None]
    for s, tile in enumerate(tiles):
        total = jnp.where(found == s, tile[None], total)
    return total.reshape(2 * P_SIZE, -1)


def exchange(amplitudes, integrals, contract_class, column_class):
    rows = amplitudes.shape[0]

    def doubled(name, value, *others):
        return jnp.concatenate([value, swap(name, value, *others)])

    own = amplitudes
    z2 = cross_z("z2", own, (2, 2))
    z1 = cross_z("z1", own, (1, 1))
    pair0 = doubled("swap0", own)
    up0 = ring("up0", pair0)
    quarter, near, far, across = cut(integrals)
    near = jnp.concatenate([near, swap("r0", far)])
    near = cross_x("r1", near, (1, 3))
    across = cross_x("r2", across, (2, 2))
    table = make_table(contract_class, column_class)
    far0 = ring("far0", up0[:rows])

    line = jnp.concatenate([z1, z2])
    turned = swap("turned", line)
    up12 = ring("up12", jnp.concatenate([line, turned]))
    z3 = cross_z("z3", z2, (1, 1))
    tiles = [quarter, near[:P_SIZE], near[P_SIZE:], across]
    merged = merge(table, tiles)
    width = merged.shape[1] // 2
    part = merged[:, :width] + swap("c1", merged[:, width:])

    pair3 = doubled("swap3", z3, turned)
    up3 = ring("up3", pair3, up12)
    moved = send("zh", part, "zh", [(0, 1), (1, 0)], turned)
    part = part + moved
    far1 = cross_z("far1", far0, (1, 1))
    far2 = ring("far2", up12[rows : 2 * rows])

    pair = doubled("c2", part)
    near = cross_x("g1", pair, (1, 3), moved)
    across = cross_x("g2", part, (2, 2))
    down = jnp.concatenate([up0[rows:], up12[2 * rows :]])
    down = swap("down", down)
    far3 = ring("far3", up3[:rows], far2)
    down3 = swap("down3", up3[rows:])
    both = jnp.concatenate([near, across])
    both_swapped = swap("c34", both)
    parts = [pair, both, both_swapped]
    pieces = [(own, 0), (line, 0), (line, rows), (z3, 0)]
    pieces += [(up0, 0), (down, 0), (far0, 0)]
    pieces += [(up12, 0), (down, rows), (far1, 0)]
    pieces += [(up12, rows), (down, 2 * rows), (far2, 0)]
    pieces += [(up3, 0), (down3, 0), (far3, 0)]
    return table, pieces, parts


def multiply_kernel(spots, table, *refs):
    count = len(refs) - 4
    pieces, parts = refs[: count - 3], refs[count - 3 : count]
    out, amps, slab, sems = refs[count:]
    rows = amps.shape[1]

    @pl.when(pl.program_id(0) == 0)
    def _():
        copies = []
        for i, (which, start) in enumerate(spots):
            source = pieces[which].at[pl.ds(start, rows)]
            copies.append(pltpu.make_async_copy(source, amps.at[i], sems.at[i]))
        place = 0
        for i, part in enumerate(parts):
            size = part.shape[0]
            target = slab.at[pl.ds(place, size)]
            copies.append(pltpu.make_async_copy(part, target, sems.at[NK + i]))
            place += size
        for copy in copies:
            copy.start()
        for copy in copies:
            copy.wait()

    block = pl.ds(pl.multiple_of(pl.program_id(0) * STEP, STEP), STEP)
    depth = 2 * P_SIZE
    for l in range(NK):
        pair = jnp.concatenate(
            [amps[table[SLOTS + r * NK + l], block] for r in range(2)], axis=1
        )
        place = pl.multiple_of(table[HALVES + l // 2] * depth, depth)
        lane = (l % 2) * P_SIZE
        weights = slab[pl.ds(place, depth), lane : lane + P_SIZE]
        out[:, l * P_SIZE : (l + 1) * P_SIZE] = jnp.dot(
            pair, weights, preferred_element_type=jnp.float32
        )


def multiply(table, pieces, parts):
    rows = pieces[0][0].shape[0]
    arrays, spots = [], []
    for piece, start in pieces:
        if not any(piece is array for array in arrays):
            arrays.append(piece)
        which = [piece is array for array in arrays].index(True)
        spots.append((which, start))
    width = NK * P_SIZE
    return pl.pallas_call(
        functools.partial(multiply_kernel, tuple(spots)),
        out_shape=jax.ShapeDtypeStruct((rows, width), jnp.float32),
        grid_spec=pltpu.PrefetchScalarGridSpec(
            num_scalar_prefetch=1,
            grid=(rows // STEP,),
            in_specs=[ANY] * (len(arrays) + len(parts)),
            out_specs=pl.BlockSpec((STEP, width), lambda i, table: (i, 0)),
            scratch_shapes=[
                pltpu.VMEM((NK, rows, P_SIZE), jnp.bfloat16),
                pltpu.VMEM((2 * NK * P_SIZE // 2, 2 * P_SIZE), jnp.bfloat16),
                pltpu.SemaphoreType.DMA((NK + len(parts),)),
            ],
        ),
        compiler_params=pltpu.CompilerParams(vmem_limit_bytes=24 * 1024 * 1024),
        cost_estimate=pl.CostEstimate(
            flops=4 * rows * P_SIZE * width,
            bytes_accessed=4 * rows * width,
            transcendentals=0,
        ),
    )(table, *arrays, *parts)


def body(amplitudes, integrals, contract_class, column_class):
    table, pieces, parts = exchange(
        amplitudes, integrals, contract_class, column_class
    )
    return multiply(table, pieces, parts)


def solution(mesh):
    fine = Mesh(mesh.devices.reshape(NX, 2, 2, NY, NZ), OCC + VIR)
    placed = (P(OCC, VIR), P(OCC, VIR), P(), P(VIR))
    return jax.shard_map(
        body, mesh=fine, in_specs=placed, out_specs=P(OCC, VIR), check_vma=False
    )
```

```python
import functools

import jax
import jax.numpy as jnp
from jax import lax
from jax.experimental import pallas as pl
from jax.experimental.pallas import tpu as pltpu
from jax.sharding import Mesh, PartitionSpec as P

P_SIZE = 128
SYMS = 8
OCC = ("x", "zh", "core")
VIR = ("y", "zl")
NX = NY = NZ = 4
NK = 16
QUARTER = 4
STEP = 256

SLOTS = 0
MERGE = 2 * NK
HALVES = MERGE + 2 * QUARTER
TABLE = HALVES + 2 * QUARTER

VMEM = pl.BlockSpec(memory_space=pltpu.VMEM)
SMEM = pl.BlockSpec(memory_space=pltpu.SMEM)
ANY = pl.BlockSpec(memory_space=pl.ANY)


def send(name, value, axes, pairs, *others):
    with jax.named_scope(name):
        if others:
            value = lax.optimization_barrier((value, *others))[0]
        return lax.ppermute(value, axes, pairs)


def swap(name, value, *others):
    return send(name, value, "core", [(0, 1), (1, 0)], *others)


def ring(name, value, *others):
    pairs = []
    for y in range(NY):
        pairs += [(y, (y + 1) % NY), (NY + y, NY + (y - 1) % NY)]
    return send(name, value, ("core", "y"), pairs, *others)


def cross_x(name, value, bits, *others):
    pairs = [(2 * x + c, 2 * (x ^ bits[c]) + c) for x in range(NX) for c in range(2)]
    return send(name, value, ("x", "core"), pairs, *others)


def after(value, *others):
    return lax.optimization_barrier((value, *others))[0]


def cross_z(name, value, bits, *others):
    pairs = [(NZ * c + z, NZ * c + (z ^ bits[c])) for z in range(NZ) for c in range(2)]
    return send(name, value, ("core", "zl"), pairs, *others)


def table_kernel(contract, column, out, inverse, rank, chosen):
    x, zh, c = (lax.axis_index(axis) for axis in OCC)
    y, z = (lax.axis_index(axis) for axis in VIR)
    one, two = (y + 3 + 2 * c) % NY, (y + 1 + 2 * c) % NY
    far = (y + 2) % NY
    sources = [(y, z), (y, z ^ 1), (y, z ^ 2), (y, z ^ 3)]
    for bit in range(NZ):
        sources += [(one, z ^ bit), (two, z ^ bit), (far, z ^ bit)]
    for i, (row, col) in enumerate(sources):
        inverse[row * NZ + col] = i
    for s in range(SYMS):
        chosen[2 * SYMS + s] = 0
    for k in range(NK):
        label = contract[k]
        place = chosen[2 * SYMS + label]
        rank[k] = place
        chosen[2 * label + place] = inverse[k]
        chosen[2 * SYMS + label] = place + 1
    for l in range(NK):
        for r in range(2):
            out[SLOTS + r * NK + l] = chosen[2 * column[l] + r]

    near_x, far_x = x ^ (1 + 2 * c), x ^ (3 - 2 * c)
    tiles = [
        x * 4 + zh * 2 + c,
        near_x * 4 + zh * 2 + c,
        near_x * 4 + zh * 2 + 1 - c,
        (x ^ 2) * 4 + zh * 2 + c,
    ]
    for j in range(QUARTER):
        half = c if j < 2 else 1 - c
        label = column[QUARTER * x + 2 * half + j % 2]
        for r in range(2):
            found = jnp.int32(len(tiles))
            for s, tile in enumerate(tiles):
                hit = (contract[tile] == label) & (rank[tile] == r)
                found = jnp.where(hit, s, found)
            out[MERGE + r * QUARTER + j] = found

    halves = [
        (x, c), (x, 1 - c),
        (near_x, c), (near_x, 1 - c),
        (x ^ 2, c),
        (far_x, 1 - c), (far_x, c),
        (x ^ 2, 1 - c),
    ]
    for i, (quarter, half) in enumerate(halves):
        out[HALVES + 2 * quarter + half] = i


def make_table(contract_class, column_class):
    return pl.pallas_call(
        table_kernel,
        out_shape=jax.ShapeDtypeStruct((TABLE,), jnp.int32),
        in_specs=[SMEM, SMEM],
        out_specs=SMEM,
        scratch_shapes=[
            pltpu.SMEM((NK,), jnp.int32),
            pltpu.SMEM((NK,), jnp.int32),
            pltpu.SMEM((3 * SYMS,), jnp.int32),
        ],
    )(contract_class, column_class)


def cut_kernel(integrals, *refs):
    outs, sems = refs[:NX], refs[NX]
    x, c = lax.axis_index("x"), lax.axis_index("core")
    half = outs[0].shape[1] // 2
    quarters = [(x, c), (x ^ (1 + 2 * c), c), (x ^ (3 - 2 * c), 1 - c), (x ^ 2, c)]
    copies = []
    for out, (quarter, first) in zip(outs, quarters):
        for i, side in enumerate((first, 1 - first)):
            start = pl.multiple_of((2 * quarter + side) * half, half)
            source = integrals.at[:, pl.ds(start, half)]
            target = out.at[:, pl.ds(i * half, half)]
            sem = sems.at[len(copies)]
            copies.append(pltpu.make_async_copy(source, target, sem))
    for copy in copies:
        copy.start()
    for copy in copies:
        copy.wait()


def cut(integrals):
    depth, width = integrals.shape
    shape = jax.ShapeDtypeStruct((depth, width // NX), integrals.dtype)
    return pl.pallas_call(
        cut_kernel,
        out_shape=[shape] * NX,
        in_specs=[ANY],
        out_specs=[VMEM] * NX,
        scratch_shapes=[pltpu.SemaphoreType.DMA((2 * NX,))],
    )(integrals)


def merge(table, tiles):
    found = table[MERGE : MERGE + 2 * QUARTER].reshape(2, 1, QUARTER)
    found = jnp.repeat(found, P_SIZE, axis=2)
    total = jnp.zeros_like(tiles[0])[None]
    for s, tile in enumerate(tiles):
        total = jnp.where(found == s, tile[None], total)
    return total.reshape(2 * P_SIZE, -1)


def exchange(amplitudes, integrals, contract_class, column_class):
    rows = amplitudes.shape[0]

    def doubled(name, value, *others):
        return jnp.concatenate([value, swap(name, value, *others)])

    own = amplitudes
    z2 = cross_z("z2", own, (2, 2))
    z1 = cross_z("z1", own, (1, 1))
    pair0 = doubled("swap0", own)
    up0 = ring("up0", pair0)
    quarter, near, far, across = cut(integrals)
    near = jnp.concatenate([near, swap("r0", far)])
    near = cross_x("r1", near, (1, 3))
    across = cross_x("r2", across, (2, 2))
    table = make_table(contract_class, column_class)
    far0 = ring("far0", up0[:rows])

    line = jnp.concatenate([z1, z2])
    turned = swap("turned", line)
    up12 = ring("up12", jnp.concatenate([line, turned]))
    z3 = cross_z("z3", z2, (1, 1))
    tiles = [quarter, near[:P_SIZE], near[P_SIZE:], across]
    merged = merge(table, tiles)
    width = merged.shape[1] // 2
    part = merged[:, :width] + swap("c1", merged[:, width:])

    pair3 = doubled("swap3", z3, turned)
    up3 = ring("up3", pair3, up12)
    moved = send("zh", part, "zh", [(0, 1), (1, 0)], turned)
    part = part + moved
    far1 = cross_z("far1", far0, (1, 1))

    pair = doubled("c2", part)
    near = cross_x("g1", pair, (1, 3), moved)
    across = cross_x("g2", part, (2, 2))
    down = jnp.concatenate([up0[rows:], up12[2 * rows :]])
    down = swap("down", down)
    both_far = jnp.concatenate([up12[rows : 2 * rows], up3[:rows]])
    far23 = ring("far23", both_far)
    down3 = swap("down3", up3[rows:])
    both = jnp.concatenate([near, across])
    both_swapped = swap("c34", both)
    parts = [pair, both, both_swapped]
    pieces = [(own, 0), (line, 0), (line, rows), (z3, 0)]
    pieces += [(up0, 0), (down, 0), (far0, 0)]
    pieces += [(up12, 0), (down, rows), (far1, 0)]
    pieces += [(up12, rows), (down, 2 * rows), (far23, 0)]
    pieces += [(up3, 0), (down3, 0), (far23, rows)]
    return table, pieces, parts


def multiply_kernel(spots, table, *refs):
    count = len(refs) - 4
    pieces, parts = refs[: count - 3], refs[count - 3 : count]
    out, amps, slab, sems = refs[count:]
    rows = amps.shape[1]

    @pl.when(pl.program_id(0) == 0)
    def _():
        copies = []
        for i, (which, start) in enumerate(spots):
            source = pieces[which].at[pl.ds(start, rows)]
            copies.append(pltpu.make_async_copy(source, amps.at[i], sems.at[i]))
        place = 0
        for i, part in enumerate(parts):
            size = part.shape[0]
            target = slab.at[pl.ds(place, size)]
            copies.append(pltpu.make_async_copy(part, target, sems.at[NK + i]))
            place += size
        for copy in copies:
            copy.start()
        for copy in copies:
            copy.wait()

    block = pl.ds(pl.multiple_of(pl.program_id(0) * STEP, STEP), STEP)
    depth = 2 * P_SIZE
    for l in range(NK):
        pair = jnp.concatenate(
            [amps[table[SLOTS + r * NK + l], block] for r in range(2)], axis=1
        )
        place = pl.multiple_of(table[HALVES + l // 2] * depth, depth)
        lane = (l % 2) * P_SIZE
        weights = slab[pl.ds(place, depth), lane : lane + P_SIZE]
        out[:, l * P_SIZE : (l + 1) * P_SIZE] = jnp.dot(
            pair, weights, preferred_element_type=jnp.float32
        )


def multiply(table, pieces, parts):
    rows = pieces[0][0].shape[0]
    arrays, spots = [], []
    for piece, start in pieces:
        if not any(piece is array for array in arrays):
            arrays.append(piece)
        which = [piece is array for array in arrays].index(True)
        spots.append((which, start))
    width = NK * P_SIZE
    return pl.pallas_call(
        functools.partial(multiply_kernel, tuple(spots)),
        out_shape=jax.ShapeDtypeStruct((rows, width), jnp.float32),
        grid_spec=pltpu.PrefetchScalarGridSpec(
            num_scalar_prefetch=1,
            grid=(rows // STEP,),
            in_specs=[ANY] * (len(arrays) + len(parts)),
            out_specs=pl.BlockSpec((STEP, width), lambda i, table: (i, 0)),
            scratch_shapes=[
                pltpu.VMEM((NK, rows, P_SIZE), jnp.bfloat16),
                pltpu.VMEM((2 * NK * P_SIZE // 2, 2 * P_SIZE), jnp.bfloat16),
                pltpu.SemaphoreType.DMA((NK + len(parts),)),
            ],
        ),
        compiler_params=pltpu.CompilerParams(vmem_limit_bytes=24 * 1024 * 1024),
        cost_estimate=pl.CostEstimate(
            flops=4 * rows * P_SIZE * width,
            bytes_accessed=4 * rows * width,
            transcendentals=0,
        ),
    )(table, *arrays, *parts)


def body(amplitudes, integrals, contract_class, column_class):
    table, pieces, parts = exchange(
        amplitudes, integrals, contract_class, column_class
    )
    return multiply(table, pieces, parts)


def solution(mesh):
    fine = Mesh(mesh.devices.reshape(NX, 2, 2, NY, NZ), OCC + VIR)
    placed = (P(OCC, VIR), P(OCC, VIR), P(), P(VIR))
    return jax.shard_map(
        body, mesh=fine, in_specs=placed, out_specs=P(OCC, VIR), check_vma=False
    )
```

```python
import functools

import jax
import jax.numpy as jnp
from jax import lax
from jax.experimental import pallas as pl
from jax.experimental.pallas import tpu as pltpu
from jax.sharding import Mesh, PartitionSpec as P

P_SIZE = 128
SYMS = 8
OCC = ("x", "zh", "core")
VIR = ("y", "zl")
NX = NY = NZ = 4
NK = 16
QUARTER = 4
STEP = 256

SLOTS = 0
MERGE = 2 * NK
HALVES = MERGE + 2 * QUARTER
TABLE = HALVES + 2 * QUARTER

VMEM = pl.BlockSpec(memory_space=pltpu.VMEM)
SMEM = pl.BlockSpec(memory_space=pltpu.SMEM)
ANY = pl.BlockSpec(memory_space=pl.ANY)


def send(name, value, axes, pairs, *others):
    with jax.named_scope(name):
        if others:
            value = lax.optimization_barrier((value, *others))[0]
        return lax.ppermute(value, axes, pairs)


def swap(name, value, *others):
    return send(name, value, "core", [(0, 1), (1, 0)], *others)


def ring(name, value, *others):
    pairs = []
    for y in range(NY):
        pairs += [(y, (y + 1) % NY), (NY + y, NY + (y - 1) % NY)]
    return send(name, value, ("core", "y"), pairs, *others)


def cross_x(name, value, bits, *others):
    pairs = [(2 * x + c, 2 * (x ^ bits[c]) + c) for x in range(NX) for c in range(2)]
    return send(name, value, ("x", "core"), pairs, *others)


def after(value, *others):
    return lax.optimization_barrier((value, *others))[0]


def cross_z(name, value, bits, *others):
    pairs = [(NZ * c + z, NZ * c + (z ^ bits[c])) for z in range(NZ) for c in range(2)]
    return send(name, value, ("core", "zl"), pairs, *others)


def table_kernel(contract, column, out, inverse, rank, chosen):
    x, zh, c = (lax.axis_index(axis) for axis in OCC)
    y, z = (lax.axis_index(axis) for axis in VIR)
    one, two = (y + 3 + 2 * c) % NY, (y + 1 + 2 * c) % NY
    far = (y + 2) % NY
    sources = [(y, z ^ bit) for bit in range(NZ)]
    sources += [(one, z), (two, z), (two, z ^ 1), (two, z ^ 2), (far, z)]
    sources += [(one, z ^ 1), (one, z ^ 2)]
    sources += [(far, z ^ 1), (far, z ^ 2), (far, z ^ 3)]
    sources += [(one, z ^ 3), (two, z ^ 3)]
    for i, (row, col) in enumerate(sources):
        inverse[row * NZ + col] = i
    for s in range(SYMS):
        chosen[2 * SYMS + s] = 0
    for k in range(NK):
        label = contract[k]
        place = chosen[2 * SYMS + label]
        rank[k] = place
        chosen[2 * label + place] = inverse[k]
        chosen[2 * SYMS + label] = place + 1
    for l in range(NK):
        for r in range(2):
            out[SLOTS + r * NK + l] = chosen[2 * column[l] + r]

    near_x, far_x = x ^ (1 + 2 * c), x ^ (3 - 2 * c)
    tiles = [
        x * 4 + zh * 2 + c,
        near_x * 4 + zh * 2 + c,
        near_x * 4 + zh * 2 + 1 - c,
        (x ^ 2) * 4 + zh * 2 + c,
    ]
    for j in range(QUARTER):
        half = c if j < 2 else 1 - c
        label = column[QUARTER * x + 2 * half + j % 2]
        for r in range(2):
            found = jnp.int32(len(tiles))
            for s, tile in enumerate(tiles):
                hit = (contract[tile] == label) & (rank[tile] == r)
                found = jnp.where(hit, s, found)
            out[MERGE + r * QUARTER + j] = found

    halves = [
        (x, c), (x, 1 - c),
        (near_x, c), (near_x, 1 - c),
        (x ^ 2, c),
        (far_x, 1 - c), (far_x, c),
        (x ^ 2, 1 - c),
    ]
    for i, (quarter, half) in enumerate(halves):
        out[HALVES + 2 * quarter + half] = i


def make_table(contract_class, column_class):
    return pl.pallas_call(
        table_kernel,
        out_shape=jax.ShapeDtypeStruct((TABLE,), jnp.int32),
        in_specs=[SMEM, SMEM],
        out_specs=SMEM,
        scratch_shapes=[
            pltpu.SMEM((NK,), jnp.int32),
            pltpu.SMEM((NK,), jnp.int32),
            pltpu.SMEM((3 * SYMS,), jnp.int32),
        ],
    )(contract_class, column_class)


def cut_kernel(integrals, *refs):
    outs, sems = refs[:NX], refs[NX]
    x, c = lax.axis_index("x"), lax.axis_index("core")
    half = outs[0].shape[1] // 2
    quarters = [(x, c), (x ^ (1 + 2 * c), c), (x ^ (3 - 2 * c), 1 - c), (x ^ 2, c)]
    copies = []
    for out, (quarter, first) in zip(outs, quarters):
        for i, side in enumerate((first, 1 - first)):
            start = pl.multiple_of((2 * quarter + side) * half, half)
            source = integrals.at[:, pl.ds(start, half)]
            target = out.at[:, pl.ds(i * half, half)]
            sem = sems.at[len(copies)]
            copies.append(pltpu.make_async_copy(source, target, sem))
    for copy in copies:
        copy.start()
    for copy in copies:
        copy.wait()


def cut(integrals):
    depth, width = integrals.shape
    shape = jax.ShapeDtypeStruct((depth, width // NX), integrals.dtype)
    return pl.pallas_call(
        cut_kernel,
        out_shape=[shape] * NX,
        in_specs=[ANY],
        out_specs=[VMEM] * NX,
        scratch_shapes=[pltpu.SemaphoreType.DMA((2 * NX,))],
    )(integrals)


def merge(table, tiles):
    found = table[MERGE : MERGE + 2 * QUARTER].reshape(2, 1, QUARTER)
    found = jnp.repeat(found, P_SIZE, axis=2)
    total = jnp.zeros_like(tiles[0])[None]
    for s, tile in enumerate(tiles):
        total = jnp.where(found == s, tile[None], total)
    return total.reshape(2 * P_SIZE, -1)


def exchange(amplitudes, integrals, contract_class, column_class):
    rows = amplitudes.shape[0]

    def doubled(name, value, *others):
        return jnp.concatenate([value, swap(name, value, *others)])

    own = amplitudes
    z2 = cross_z("z2", own, (2, 2))
    z1 = cross_z("z1", own, (1, 1))
    pair0 = doubled("swap0", own)
    up0 = ring("up0", pair0)
    quarter, near, far, across = cut(integrals)
    near = jnp.concatenate([near, swap("r0", far)])
    near = cross_x("r1", near, (1, 3))
    across = cross_x("r2", across, (2, 2))
    table = make_table(contract_class, column_class)
    far0 = ring("far0", up0[:rows])

    line = jnp.concatenate([z1, z2])
    turned = swap("turned", line)
    up12 = ring("up12", jnp.concatenate([line, turned]))
    z3 = cross_z("z3", z2, (1, 1))
    tiles = [quarter, near[:P_SIZE], near[P_SIZE:], across]
    merged = merge(table, tiles)
    width = merged.shape[1] // 2
    part = merged[:, :width] + swap("c1", merged[:, width:])

    pair3 = doubled("swap3", z3, turned)
    up3 = ring("up3", pair3, up12)
    moved = send("zh", part, "zh", [(0, 1), (1, 0)], turned)
    part = part + moved
    far1 = cross_z("far1", far0, (1, 1))

    pair = doubled("c2", part)
    near = cross_x("g1", pair, (1, 3), moved)
    across = cross_x("g2", part, (2, 2))
    down = jnp.concatenate([up0[rows:], up12[2 * rows :]])
    down = swap("down", down)
    both_far = jnp.concatenate([up12[rows : 2 * rows], up3[:rows]])
    far23 = ring("far23", both_far)
    down3 = swap("down3", up3[rows:])
    both = jnp.concatenate([near, across])
    both_swapped = swap("c34", both)
    parts = [pair, both, both_swapped]
    pieces = [(own, 0), (line, 0), (line, rows), (z3, 0)]
    pieces += [(up0, 0), (down, 0), (down, rows), (down, 2 * rows), (far0, 0)]
    pieces += [(up12, 0), (up12, rows), (far1, 0), (far23, 0), (far23, rows)]
    pieces += [(up3, 0), (down3, 0)]
    return table, pieces, parts


def multiply_kernel(spots, table, *refs):
    count = len(refs) - 4
    pieces, parts = refs[: count - 3], refs[count - 3 : count]
    out, amps, slab, sems = refs[count:]
    rows = amps.shape[0] // NK

    @pl.when(pl.program_id(0) == 0)
    def _():
        copies = []
        i = 0
        while i < NK:
            which, start = spots[i]
            run = 1
            while i + run < NK and spots[i + run] == (which, start + run * rows):
                run += 1
            source = pieces[which].at[pl.ds(start, run * rows)]
            target = amps.at[pl.ds(i * rows, run * rows)]
            copies.append(pltpu.make_async_copy(source, target, sems.at[i]))
            i += run
        place = 0
        for i, part in enumerate(parts):
            size = part.shape[0]
            target = slab.at[pl.ds(place, size)]
            copies.append(pltpu.make_async_copy(part, target, sems.at[NK + i]))
            place += size
        for copy in copies:
            copy.start()
        for copy in copies:
            copy.wait()

    shift = pl.program_id(0) * STEP
    depth = 2 * P_SIZE
    for l in range(NK):
        starts = [
            pl.multiple_of(table[SLOTS + r * NK + l] * rows + shift, STEP) for r in range(2)
        ]
        pair = jnp.concatenate([amps[pl.ds(start, STEP)] for start in starts], axis=1)
        place = pl.multiple_of(table[HALVES + l // 2] * depth, depth)
        lane = (l % 2) * P_SIZE
        weights = slab[pl.ds(place, depth), lane : lane + P_SIZE]
        out[:, l * P_SIZE : (l + 1) * P_SIZE] = jnp.dot(
            pair, weights, preferred_element_type=jnp.float32
        )


def multiply(table, pieces, parts):
    rows = pieces[0][0].shape[0]
    arrays, spots = [], []
    for piece, start in pieces:
        if not any(piece is array for array in arrays):
            arrays.append(piece)
        which = [piece is array for array in arrays].index(True)
        spots.append((which, start))
    width = NK * P_SIZE
    return pl.pallas_call(
        functools.partial(multiply_kernel, tuple(spots)),
        out_shape=jax.ShapeDtypeStruct((rows, width), jnp.float32),
        grid_spec=pltpu.PrefetchScalarGridSpec(
            num_scalar_prefetch=1,
            grid=(rows // STEP,),
            in_specs=[ANY] * (len(arrays) + len(parts)),
            out_specs=pl.BlockSpec((STEP, width), lambda i, table: (i, 0)),
            scratch_shapes=[
                pltpu.VMEM((NK * rows, P_SIZE), jnp.bfloat16),
                pltpu.VMEM((2 * NK * P_SIZE // 2, 2 * P_SIZE), jnp.bfloat16),
                pltpu.SemaphoreType.DMA((NK + len(parts),)),
            ],
        ),
        compiler_params=pltpu.CompilerParams(vmem_limit_bytes=24 * 1024 * 1024),
        cost_estimate=pl.CostEstimate(
            flops=4 * rows * P_SIZE * width,
            bytes_accessed=4 * rows * width,
            transcendentals=0,
        ),
    )(table, *arrays, *parts)


def body(amplitudes, integrals, contract_class, column_class):
    table, pieces, parts = exchange(
        amplitudes, integrals, contract_class, column_class
    )
    return multiply(table, pieces, parts)


def solution(mesh):
    fine = Mesh(mesh.devices.reshape(NX, 2, 2, NY, NZ), OCC + VIR)
    placed = (P(OCC, VIR), P(OCC, VIR), P(), P(VIR))
    return jax.shard_map(
        body, mesh=fine, in_specs=placed, out_specs=P(OCC, VIR), check_vma=False
    )
```
